32 devices in a mesh: rows: 4 (over x, core), cols: 8 (over z, y).
Axes of the slice: x: 2, y: 2, z: 4, core: 2. Of those that a mesh axis runs over, the one named last changes fastest.
Arguments:
- slab: float32 [32768, 2048], P('rows', 'cols'), may hold values from -6 to 6
- sign_bits: int32 [32768], P('rows'), may hold values from 0 to 1
- sample_rows: int32 [4096], replicated, may hold values from 0 to 32767, as said below
Outputs:
- gram: float32 [2048, 2048], P('rows', 'cols')
The draws below stay inside these ranges and needn't reach their ends.
Inputs may be any that keep to these rules, and one draw needn't show every extreme that they name: `sample_rows`: Ascending; repeats may occur. At most 2048 indices fall in any one device's aligned block of 8192 rows, and some block holds exactly 2048.
All inputs are finite; a program needn't handle non-finite values.
Results may differ from the reference program's by a relative error of at most 0.000071.
Values sent between devices are 32-bit elements; how exact they have to be, the bound alone decides.
No kernel may reach another device: no remote copies, remote signals or barrier semaphores. Data moves between devices by JAX's collectives and lax.ppermute only.
A program may use at most 64 MiB of HBM per device.

```python
import jax
import jax.numpy as jnp
from jax import lax

D = 2048
ROWS_DEV = 8192
SAMP = 1024
M = 32768
SAMPLES = 4096
N_ROWS = 4


def draw_sample_rows(key, part):
    first_key, second_key, third_key = jax.random.split(key, 3)
    pairs = N_ROWS // 2
    excess = jax.random.randint(first_key, (pairs,), 0, SAMP + 1).astype(jnp.int32)
    excess = excess.at[0].set(SAMP)
    paired = jnp.stack([SAMP + excess, SAMP - excess], axis=1).reshape(N_ROWS)
    ordering = jax.random.permutation(second_key, N_ROWS)
    counts = paired[ordering]
    bounds = jnp.cumsum(counts).astype(jnp.int32)
    slot_ids = jnp.arange(SAMPLES, dtype=jnp.int32)
    owners = jnp.sum((slot_ids[:, None] >= bounds[None, :]).astype(jnp.int32), axis=1).astype(jnp.int32)
    offset = jax.random.randint(third_key, (SAMPLES,), 0, ROWS_DEV).astype(jnp.int32)
    return jnp.sort(owners * ROWS_DEV + offset).astype(jnp.int32)


def plant(drawn, rng, least, top_value):
    index_at = [jax.random.randint(jax.random.fold_in(rng, axis), (), 0, length) for axis, length in enumerate(drawn.shape)]
    widest = drawn.shape.index(max(drawn.shape))
    neighbour = index_at[:widest] + [(index_at[widest] + 1) % drawn.shape[widest]] + index_at[widest + 1:]
    return drawn.at[tuple(index_at)].set(least).at[tuple(neighbour)].set(top_value)


def block_scale(own_key, dims, shards, low, high):
    factor_of = 1.0
    for axis_at, shards_of in shards:
        heights = jax.random.uniform(jax.random.fold_in(jax.random.fold_in(own_key, 6), axis_at), (shards_of,), jnp.float32, low / len(shards), high / len(shards))
        factor_of = factor_of * jnp.repeat(jnp.exp(heights), dims[axis_at] // shards_of).reshape((-1,) + (1,) * (len(dims) - 1 - axis_at))
    return factor_of


def normal_values(rng, extent, scale, reach, shards=(), kind=jnp.bfloat16):
    values = scale * jax.random.normal(rng, extent, jnp.float32)
    if shards:
        values = values * block_scale(rng, extent, shards, -0.22, 0.18)
    return jnp.clip(values, -reach, reach).astype(kind)


def setup_inputs(seed: int = 0) -> dict:
    seeds = jax.random.split(jax.random.key(seed), 4)
    slab = normal_values(seeds[0], (M, D), 1.0, 6.0, ((0, 4), (1, 8)), jnp.float32)
    sign_bits = plant(jax.random.randint(seeds[1], (M,), 0, 2), jax.random.fold_in(seeds[1], 1), 0, 1).astype(jnp.int32)
    sample_rows = draw_sample_rows(jax.random.fold_in(seeds[3], 71), 0)
    return dict(slab=slab, sign_bits=sign_bits, sample_rows=sample_rows)


def parity_table(length):
    index_list = jnp.arange(length, dtype=jnp.int32)
    common = index_list[:, None] & index_list[None, :]
    parity = jnp.zeros((length, length), jnp.int32)
    for bit_number in range(max(length.bit_length() - 1, 0)):
        parity = parity + ((common >> bit_number) & 1)
    return (1 - 2 * (parity % 2)).astype(jnp.float32)


def reference(slab, sign_bits, sample_rows):
    flipped = slab * (1 - 2 * sign_bits).astype(jnp.float32)[:, None]
    blocks = flipped.reshape(M // 128, 128, D)
    mixed = jnp.einsum("ij,qjc->qic", parity_table(128), blocks, precision=lax.Precision.HIGHEST)
    outer_count = M // 128
    stride = 1
    while stride < outer_count:
        shaped = mixed.reshape(outer_count // (2 * stride), 2, stride, 128, D)
        first_half = shaped[:, 0]
        second_half = shaped[:, 1]
        mixed = jnp.stack([first_half + second_half, first_half - second_half], axis=1)
        stride = stride * 2
    mixed = mixed.reshape(M, D)
    picked = jnp.take(mixed, sample_rows, axis=0)
    gram = jnp.dot(picked.T, picked, precision=lax.Precision.HIGHEST, preferred_element_type=jnp.float32)
    return gram * (1.0 / (SAMPLES * M))
```

```python
import functools

import jax
import jax.numpy as jnp
from jax import lax
from jax.experimental import pallas as pl
from jax.experimental.pallas import tpu as pltpu
from jax.sharding import PartitionSpec as P

LANES = 128
INNER = 128
AXES = ("rows", "cols")


def bit_reverse(value, bits):
    return sum(((value >> at) & 1) << (bits - 1 - at) for at in range(bits))


def butterflies(parts):
    stride = 1
    while stride < len(parts):
        for at in range(len(parts)):
            if not at & stride:
                low, high = parts[at], parts[at + stride]
                parts[at], parts[at + stride] = low + high, low - high
        stride *= 2
    return parts


def transform_and_pick(groups, me_ref, index_ref, slab_ref, flip_ref, keep_ref, send_ref, mixed):
    step, steps = pl.program_id(0), mixed.shape[0] // 2 // slab_ref.shape[0]
    block = slab_ref.shape[0]
    height = block * steps
    base = step * block

    row = lax.broadcasted_iota(jnp.int32, (INNER, 2 * INNER), 0)
    col = lax.broadcasted_iota(jnp.int32, (INNER, 2 * INNER), 1) & (INNER - 1)
    common = row & col
    for shift in (4, 2, 1):
        common = common ^ (common >> shift)
    table = (1 - 2 * (common & 1)).astype(jnp.float32)

    inner_blocks = block // INNER
    for at in range(inner_blocks):
        flip = flip_ref[0, at : at + 1, :]
        signed = (table * jnp.concatenate([flip, flip], axis=1)).astype(jnp.bfloat16)
        values = slab_ref[at * INNER : (at + 1) * INNER, :]
        high = values.astype(jnp.bfloat16)
        low = (values - high.astype(jnp.float32)).astype(jnp.bfloat16)
        mixed[pl.ds(pl.multiple_of(base + at * INNER, INNER), INNER), :] = jnp.dot(
            signed, jnp.concatenate([high, low], axis=0), preferred_element_type=jnp.float32
        )

    def combine(starts, negate):
        parts = butterflies([mixed[pl.ds(pl.multiple_of(s, 8), 8), :] for s in starts])
        for s, part in zip(starts, parts):
            mixed[pl.ds(pl.multiple_of(s, 8), 8), :] = part
            if negate:
                mixed[pl.ds(pl.multiple_of(s + height, 8), 8), :] = -part

    @pl.loop(0, INNER // 8, unroll=4)
    def _(tile):
        combine([base + at * INNER + tile * 8 for at in range(inner_blocks)], False)

    @pl.when(step == steps - 1)
    def _():
        @pl.loop(0, block // 8, unroll=4)
        def _(tile):
            combine([at * block + tile * 8 for at in range(steps)], True)

        count = index_ref.shape[0] // groups
        bits = groups.bit_length() - 1
        half = max(groups // 2, 1)
        for place in range(groups):
            out = keep_ref if place < half else send_ref
            start = (me_ref[0] ^ bit_reverse(place, bits)) * count
            to = (place % half) * count

            @pl.loop(0, count // 16)
            def _(chunk):
                for at in range(16):
                    source = index_ref[start + chunk * 16 + at]
                    out[pl.ds(to + chunk * 16 + at, 1), :] = mixed[pl.ds(source, 1), :]


def picked_strip(slab, flips, index, me, groups, strip):
    height = slab.shape[0]
    samples = index.shape[0]
    block = min(1024, height)
    half = jax.ShapeDtypeStruct((samples // 2, LANES), jnp.float32)
    return pl.pallas_call(
        functools.partial(transform_and_pick, groups),
        out_shape=(half, half),
        grid_spec=pltpu.PrefetchScalarGridSpec(
            num_scalar_prefetch=2,
            grid=(height // block,),
            in_specs=[
                pl.BlockSpec((block, LANES), lambda step, *_: (step, strip)),
                pl.BlockSpec((1, block // INNER, INNER), lambda step, *_: (step, 0, 0)),
            ],
            out_specs=[pl.BlockSpec((samples // 2, LANES), lambda step, *_: (0, 0))] * 2,
            scratch_shapes=[pltpu.VMEM((2 * height, LANES), jnp.float32)],
        ),
        compiler_params=pltpu.CompilerParams(vmem_limit_bytes=40 * 1024 * 1024),
        cost_estimate=pl.CostEstimate(
            flops=4 * height * INNER * LANES, bytes_accessed=4 * LANES * (height + samples), transcendentals=0
        ),
        name="transform_and_pick",
    )(me, index, slab, flips)


def column_product(portion, own_rows):
    return lax.dot_general(
        portion,
        own_rows,
        (((0,), (0,)), ((), ())),
        precision=lax.Precision.HIGH,
        preferred_element_type=jnp.float32,
    )


def shards(slab, sign_bits, sample_rows):
    height, width = slab.shape
    groups = lax.axis_size("rows")
    me = lax.axis_index("rows")
    samples = sample_rows.shape[0]
    factor = 1.0 / (samples * height * groups)
    bits = groups.bit_length() - 1

    owners = sample_rows // height
    common = owners & me
    parity = jnp.zeros_like(common)
    for at in range(bits):
        parity = parity ^ ((common >> at) & 1)
    index = sample_rows - owners * height + parity * height
    block = min(1024, height)
    flips = (1 - 2 * sign_bits).astype(jnp.float32).reshape(height // block, block // INNER, INNER)
    me_array = me.reshape(1)

    strips = []
    for strip in range(width // LANES):
        keep, send = picked_strip(slab, flips, index, me_array, groups, strip)
        for at in range(bits):
            pairs = [(r, r ^ (1 << at)) for r in range(groups)]
            got = lax.ppermute(send, "rows", pairs)
            half = keep.shape[0] // 2
            if at < bits - 1:
                keep, send = keep[:half] + got[:half], keep[half:] + got[half:]
            else:
                keep = keep + got
        strips.append(keep)
    own_rows = jnp.concatenate(strips, axis=1)
    terms = column_product(lax.all_gather(own_rows, "cols", axis=1, tiled=True), own_rows)
    return lax.psum_scatter(terms * factor, "rows", scatter_dimension=0, tiled=True)


def solution(mesh):
    return jax.shard_map(
        shards,
        mesh=mesh,
        in_specs=(P("rows", "cols"), P("rows"), P()),
        out_specs=P("rows", "cols"),
        check_vma=False,
    )
```

```python
import functools

import jax
import jax.numpy as jnp
from jax import lax
from jax.experimental import pallas as pl
from jax.experimental.pallas import tpu as pltpu
from jax.sharding import PartitionSpec as P

LANES = 128
INNER = 128
AXES = ("rows", "cols")


def bit_reverse(value, bits):
    return sum(((value >> at) & 1) << (bits - 1 - at) for at in range(bits))


def butterflies(parts):
    stride = 1
    while stride < len(parts):
        for at in range(len(parts)):
            if not at & stride:
                low, high = parts[at], parts[at + stride]
                parts[at], parts[at + stride] = low + high, low - high
        stride *= 2
    return parts


def transform_and_pick(groups, me_ref, index_ref, slab_ref, flip_ref, keep_ref, send_ref, mixed):
    step, steps = pl.program_id(0), mixed.shape[0] // 2 // slab_ref.shape[0]
    block = slab_ref.shape[0]
    height = block * steps
    base = step * block

    row = lax.broadcasted_iota(jnp.int32, (INNER, 2 * INNER), 0)
    col = lax.broadcasted_iota(jnp.int32, (INNER, 2 * INNER), 1) & (INNER - 1)
    common = row & col
    for shift in (4, 2, 1):
        common = common ^ (common >> shift)
    table = (1 - 2 * (common & 1)).astype(jnp.float32)

    inner_blocks = block // INNER
    for at in range(inner_blocks):
        flip = flip_ref[0, at : at + 1, :]
        signed = (table * jnp.concatenate([flip, flip], axis=1)).astype(jnp.bfloat16)
        values = slab_ref[at * INNER : (at + 1) * INNER, :]
        high = values.astype(jnp.bfloat16)
        low = (values - high.astype(jnp.float32)).astype(jnp.bfloat16)
        mixed[pl.ds(pl.multiple_of(base + at * INNER, INNER), INNER), :] = jnp.dot(
            signed, jnp.concatenate([high, low], axis=0), preferred_element_type=jnp.float32
        )

    def combine(starts, negate):
        parts = butterflies([mixed[pl.ds(pl.multiple_of(s, 8), 8), :] for s in starts])
        for s, part in zip(starts, parts):
            mixed[pl.ds(pl.multiple_of(s, 8), 8), :] = part
            if negate:
                mixed[pl.ds(pl.multiple_of(s + height, 8), 8), :] = -part

    @pl.loop(0, INNER // 8, unroll=4)
    def _(tile):
        combine([base + at * INNER + tile * 8 for at in range(inner_blocks)], False)

    @pl.when(step == steps - 1)
    def _():
        @pl.loop(0, block // 8, unroll=4)
        def _(tile):
            combine([at * block + tile * 8 for at in range(steps)], True)

        count = index_ref.shape[0] // groups
        bits = groups.bit_length() - 1
        half = max(groups // 2, 1)
        for place in range(groups):
            out = keep_ref if place < half else send_ref
            start = (me_ref[0] ^ bit_reverse(place, bits)) * count
            to = (place % half) * count

            @pl.loop(0, count // 16)
            def _(chunk):
                for at in range(16):
                    source = index_ref[start + chunk * 16 + at]
                    out[pl.ds(to + chunk * 16 + at, 1), :] = mixed[pl.ds(source, 1), :]


def picked_strip(slab, flips, index, me, groups, strip):
    height = slab.shape[0]
    samples = index.shape[0]
    block = min(1024, height)
    half = jax.ShapeDtypeStruct((samples // 2, LANES), jnp.float32)
    return pl.pallas_call(
        functools.partial(transform_and_pick, groups),
        out_shape=(half, half),
        grid_spec=pltpu.PrefetchScalarGridSpec(
            num_scalar_prefetch=2,
            grid=(height // block,),
            in_specs=[
                pl.BlockSpec((block, LANES), lambda step, *_: (step, strip)),
                pl.BlockSpec((1, block // INNER, INNER), lambda step, *_: (step, 0, 0)),
            ],
            out_specs=[pl.BlockSpec((samples // 2, LANES), lambda step, *_: (0, 0))] * 2,
            scratch_shapes=[pltpu.VMEM((2 * height, LANES), jnp.float32)],
        ),
        compiler_params=pltpu.CompilerParams(vmem_limit_bytes=40 * 1024 * 1024),
        cost_estimate=pl.CostEstimate(
            flops=4 * height * INNER * LANES, bytes_accessed=4 * LANES * (height + samples), transcendentals=0
        ),
        name="transform_and_pick",
    )(me, index, slab, flips)


def two_parts(values):
    high = values.astype(jnp.bfloat16)
    return high, (values - high.astype(jnp.float32)).astype(jnp.bfloat16)


def three_products(left, right):
    dot = functools.partial(jnp.dot, preferred_element_type=jnp.float32)
    return dot(left[0], right[0]) + dot(left[0], right[1]) + dot(left[1], right[0])


def pair_products(groups, near, strips, spot_ref, *refs):
    refs = list(refs)

    def take(count):
        taken, refs[:count] = refs[:count], []
        return taken

    plane = [[take(strips) for _ in range(2)] for _ in range(near)]
    remote = [[take(strips) for _ in range(2)] for _ in range(groups - 1)]
    keep_ref, send_ref, turned_high, turned_low = refs
    me, at_plane, at_near = spot_ref[0], spot_ref[1], spot_ref[2]
    half, width = keep_ref.shape[0], keep_ref.shape[2]
    depth = plane[0][0][0].shape[0]
    bits = groups.bit_length() - 1

    def whole(parts):
        return jnp.concatenate([part[...] for part in parts], axis=1)

    for off in range(near):
        rows = pl.ds(pl.multiple_of((at_near ^ off) * width, width), width)
        for side in range(2):
            for strip in range(strips):
                high, low = two_parts(plane[off][side][strip][...].T)
                where = pl.ds(pl.multiple_of((at_near ^ off) * width + strip * LANES, LANES), LANES)
                turned_high[side, where, :] = high
                turned_low[side, where, :] = low

    def store(other, value):
        place = bit_reverse(other ^ me, bits)

        @pl.when(place < half)
        def _():
            keep_ref[place] = value

        @pl.when(place >= half)
        def _():
            send_ref[place - half] = value

    def product(side, parts):
        return three_products((turned_high[side], turned_low[side]), two_parts(whole(parts)))

    store(at_plane, product(0, plane[0][0]) + product(1, plane[0][1]))
    for away in range(1, groups):
        for side in range(2):
            other = at_plane - away if side == 0 else at_plane + away

            @pl.when((other >= 0) & (other < groups))
            def _():
                store(other, product(side, remote[away - 1][side]))


def finish(factor, spot_ref, total_ref, direct_ref, *refs):
    out_ref, turned = refs[-1], refs[:-1]
    me, at_plane, at_near = spot_ref[0], spot_ref[1], spot_ref[2]
    width = out_ref.shape[1]

    @pl.when(me == at_plane)
    def _():
        out_ref[...] = total_ref[...] * factor

    @pl.when(me != at_plane)
    def _():
        for off in range(len(turned) + 1):
            rows = pl.ds(pl.multiple_of((at_near ^ off) * width, width), width)
            part = total_ref[rows, :] if off == 0 else turned[off - 1][...]
            out_ref[rows, :] = (direct_ref[rows, :] + part.T) * factor


def shards(slab, sign_bits, sample_rows):
    height, width = slab.shape
    groups, columns = lax.axis_size("rows"), lax.axis_size("cols")
    near = columns // groups
    me, column = lax.axis_index("rows"), lax.axis_index("cols")
    samples = sample_rows.shape[0]
    factor = 1.0 / (samples * height * groups)
    bits = groups.bit_length() - 1

    owners = sample_rows // height
    common = owners & me
    parity = jnp.zeros_like(common)
    for at in range(bits):
        parity = parity ^ ((common >> at) & 1)
    index = sample_rows - owners * height + parity * height
    block = min(1024, height)
    flips = (1 - 2 * sign_bits).astype(jnp.float32).reshape(height // block, block // INNER, INNER)
    spot = jnp.stack([me, column // near, column % near]).astype(jnp.int32)

    def halve(keep, send, at):
        got = lax.ppermute(send, "rows", [(r, r ^ (1 << at)) for r in range(groups)])
        half = keep.shape[0] // 2
        if at == bits - 1:
            return keep, got
        return keep[:half] + got[:half], keep[half:] + got[half:]

    strips = width // LANES
    plane = [[[] for _ in range(2)] for _ in range(near)]
    remote = [[[] for _ in range(2)] for _ in range(groups - 1)]
    for strip in range(strips):
        keep, send = picked_strip(slab, flips, index, spot, groups, strip)
        for at in range(bits):
            keep, send = halve(keep, send, at)
        half = keep.shape[0] // 2
        own = [keep[:half] + send[:half], keep[half:] + send[half:]]
        moving = list(own)
        for away in range(1, groups):
            moving[0] = lax.ppermute(moving[0], "cols", [(c, c + near) for c in range((away - 1) * near, columns - near)])
            moving[1] = lax.ppermute(moving[1], "cols", [(c, c - near) for c in range(near, columns - (away - 1) * near)])
            for side in range(2):
                remote[away - 1][side].append(moving[side])
        for side in range(2):
            plane[0][side].append(own[side])
            for off in range(1, near):
                plane[off][side].append(lax.ppermute(own[side], "cols", [(c, c ^ off) for c in range(columns)]))

    operands = [part for group in plane + remote for side in group for part in side]
    depth = operands[0].shape[0]
    half_sums = jax.ShapeDtypeStruct((groups // 2, near * width, width), jnp.float32)
    vmem = pl.BlockSpec(memory_space=pltpu.VMEM)
    smem = pl.BlockSpec(memory_space=pltpu.SMEM)
    keep, send = pl.pallas_call(
        functools.partial(pair_products, groups, near, strips),
        out_shape=(half_sums, half_sums),
        in_specs=[smem] + [vmem] * len(operands),
        out_specs=(vmem, vmem),
        scratch_shapes=[pltpu.VMEM((2, near * width, depth), jnp.bfloat16)] * 2,
        compiler_params=pltpu.CompilerParams(vmem_limit_bytes=40 * 1024 * 1024),
        name="pair_products",
    )(spot, *operands)
    for at in range(bits):
        keep, send = halve(keep, send, at)
    total = (keep + send)[0]

    direct = lax.ppermute(
        total,
        AXES,
        [
            (r * columns + c, c // near * columns + r * near + c % near)
            for r in range(groups)
            for c in range(columns)
        ],
    )
    turned = []
    for off in range(1, near):
        part = lax.dynamic_slice_in_dim(total, (column % near ^ off) * width, width, 0)
        turned.append(lax.ppermute(part, "cols", [(c, c ^ off) for c in range(columns)]))
    return pl.pallas_call(
        functools.partial(finish, factor),
        out_shape=jax.ShapeDtypeStruct((near * width, width), jnp.float32),
        in_specs=[smem] + [vmem] * (2 + len(turned)),
        out_specs=vmem,
        compiler_params=pltpu.CompilerParams(vmem_limit_bytes=16 * 1024 * 1024),
        name="finish",
    )(spot, total, direct, *turned)


def solution(mesh):
    return jax.shard_map(
        shards,
        mesh=mesh,
        in_specs=(P("rows", "cols"), P("rows"), P()),
        out_specs=P("rows", "cols"),
        check_vma=False,
    )
```

```python
import functools

import jax
import jax.numpy as jnp
from jax import lax
from jax.experimental import pallas as pl
from jax.experimental.pallas import tpu as pltpu
from jax.sharding import PartitionSpec as P

LANES = 128
INNER = 128
AXES = ("rows", "cols")


def bit_reverse(value, bits):
    return sum(((value >> at) & 1) << (bits - 1 - at) for at in range(bits))


def butterflies(parts):
    stride = 1
    while stride < len(parts):
        for at in range(len(parts)):
            if not at & stride:
                low, high = parts[at], parts[at + stride]
                parts[at], parts[at + stride] = low + high, low - high
        stride *= 2
    return parts


def transform_and_pick(groups, strip, spot_ref, index_ref, bits_ref, slab_ref, keep_ref, send_ref, mixed, arrived):
    height = slab_ref.shape[0]
    steps = arrived.shape[0]
    block = height // steps
    inner_blocks = block // INNER

    def fetch(step):
        rows = pl.ds(pl.multiple_of(step * block, block), block)
        return pltpu.make_async_copy(
            slab_ref.at[rows, pl.ds(strip * LANES, LANES)], mixed.at[rows, :], arrived.at[step]
        )

    for step in range(steps):
        fetch(step).start()

    row = lax.broadcasted_iota(jnp.int32, (INNER, 2 * INNER), 0)
    col = lax.broadcasted_iota(jnp.int32, (INNER, 2 * INNER), 1) & (INNER - 1)
    common = row & col
    for shift in (4, 2, 1):
        common = common ^ (common >> shift)
    table = (1 - 2 * (common & 1)).astype(jnp.float32)

    def combine(starts, negate):
        parts = butterflies([mixed[pl.ds(pl.multiple_of(s, 8), 8), :] for s in starts])
        for s, part in zip(starts, parts):
            mixed[pl.ds(pl.multiple_of(s, 8), 8), :] = part
            if negate:
                mixed[pl.ds(pl.multiple_of(s + height, 8), 8), :] = -part

    @pl.loop(0, steps)
    def _(step):
        base = step * block
        fetch(step).wait()
        flips = (1 - 2 * bits_ref[step]).astype(jnp.float32)
        for at in range(inner_blocks):
            rows = pl.ds(pl.multiple_of(base + at * INNER, INNER), INNER)
            flip = flips[at : at + 1, :]
            signed = (table * jnp.concatenate([flip, flip], axis=1)).astype(jnp.bfloat16)
            mixed[rows, :] = jnp.dot(
                signed, jnp.concatenate(two_parts(mixed[rows, :]), axis=0), preferred_element_type=jnp.float32
            )

        @pl.loop(0, INNER // 8, unroll=4)
        def _(tile):
            combine([base + at * INNER + tile * 8 for at in range(inner_blocks)], False)

    @pl.loop(0, block // 8, unroll=4)
    def _(tile):
        combine([at * block + tile * 8 for at in range(steps)], True)

    count = index_ref.shape[0] // groups
    bits = groups.bit_length() - 1
    half = groups // 2
    for place in range(groups):
        out = keep_ref if place < half else send_ref
        start = (spot_ref[0] ^ bit_reverse(place, bits)) * count
        to = (place % half) * count

        @pl.loop(0, count // 32)
        def _(chunk):
            for at in range(32):
                source = index_ref[start + chunk * 32 + at]
                out[pl.ds(to + chunk * 32 + at, 1), :] = mixed[pl.ds(source, 1), :]


VMEM = pl.BlockSpec(memory_space=pltpu.VMEM)
SMEM = pl.BlockSpec(memory_space=pltpu.SMEM)
MIB = 1024 * 1024


def picked_strip(slab, sign_bits, index, spot, groups, strip):
    height = slab.shape[0]
    samples = index.shape[0]
    steps = sign_bits.shape[0]
    half = jax.ShapeDtypeStruct((samples // 2, LANES), jnp.float32)
    return pl.pallas_call(
        functools.partial(transform_and_pick, groups, strip),
        out_shape=(half, half),
        in_specs=[SMEM, SMEM, VMEM, pl.BlockSpec(memory_space=pl.ANY)],
        out_specs=(VMEM, VMEM),
        scratch_shapes=[pltpu.VMEM((2 * height, LANES), jnp.float32), pltpu.SemaphoreType.DMA((steps,))],
        compiler_params=pltpu.CompilerParams(vmem_limit_bytes=56 * MIB),
        cost_estimate=pl.CostEstimate(
            flops=16 * height * INNER * LANES, bytes_accessed=16 * LANES * (height + samples), transcendentals=0
        ),
        name="transform_and_pick",
    )(spot, index, sign_bits, slab)


def two_parts(values):
    high = values.astype(jnp.bfloat16)
    return high, (values - high.astype(jnp.float32)).astype(jnp.bfloat16)


def three_products(left, right):
    dot = functools.partial(jnp.dot, preferred_element_type=jnp.float32)
    return dot(left[0], right[0]) + dot(left[0], right[1]) + dot(left[1], right[0])


def turn_plane(near, strips, spot_ref, *refs):
    parts, (high_ref, low_ref, own_ref) = refs[:-3], refs[-3:]
    width = own_ref.shape[1]
    for off in range(near):
        for strip in range(strips):
            high, low = two_parts(parts[off * strips + strip][...].T)
            where = pl.ds(pl.multiple_of((spot_ref[2] ^ off) * width + strip * LANES, LANES), LANES)
            high_ref[where, :] = high
            low_ref[where, :] = low
    own = jnp.concatenate([part[...] for part in parts[:strips]], axis=1)
    own_ref[...] = three_products((high_ref[...], low_ref[...]), two_parts(own))


def pair_products(groups, strip, spot_ref, high_ref, low_ref, own_ref, *refs):
    remote, (keep_ref, send_ref) = refs[:-2], refs[-2:]
    me, at_plane = spot_ref[0], spot_ref[1]
    half = keep_ref.shape[0]
    bits = groups.bit_length() - 1
    back = 1 - 2 * (me & 1)

    def store(other, value):
        place = bit_reverse(other ^ me, bits)

        @pl.when(place < half)
        def _():
            keep_ref[place] = value()

        @pl.when(place >= half)
        def _():
            send_ref[place - half] = value()

    store(at_plane, lambda: own_ref[:, strip * LANES : (strip + 1) * LANES])
    for away in range(1, groups):
        below, above = at_plane - away * back, at_plane + away * back

        @pl.when((below >= 0) & (below < groups))
        def _():
            product = three_products((high_ref[...], low_ref[...]), two_parts(remote[away - 1][...]))
            store(below, lambda: product)

        @pl.when((above >= 0) & (above < groups))
        def _():
            store(above, lambda: jnp.zeros(keep_ref.shape[1:], jnp.float32))


def finish(factor, near, strips, spot_ref, *refs):
    totals, directs, turned, out_ref = refs[:strips], refs[strips : 2 * strips], refs[2 * strips : -1], refs[-1]
    me, at_plane, at_near = spot_ref[0], spot_ref[1], spot_ref[2]
    width = out_ref.shape[1]

    @pl.when(me == at_plane)
    def _():
        for strip in range(strips):
            out_ref[:, strip * LANES : (strip + 1) * LANES] = totals[strip][...] * factor

    @pl.when(me != at_plane)
    def _():
        direct = jnp.concatenate([part[...] for part in directs], axis=1) * factor
        out_ref[...] = direct
        for off in range(near):
            start = pl.multiple_of((at_near ^ off) * width, width)
            for strip in range(strips):
                part = totals[strip][pl.ds(start, width), :] if off == 0 else turned[(off - 1) * strips + strip][...]
                rows = pl.ds(pl.multiple_of(start + strip * LANES, LANES), LANES)
                out_ref[rows, :] = out_ref[rows, :] + part.T * factor


def shards(slab, sign_bits, sample_rows):
    height, width = slab.shape
    groups, columns = lax.axis_size("rows"), lax.axis_size("cols")
    near = columns // groups
    strips = width // LANES
    me, column = lax.axis_index("rows"), lax.axis_index("cols")
    samples = sample_rows.shape[0]
    factor = 1.0 / (samples * height * groups)
    bits = groups.bit_length() - 1

    owners = sample_rows // height
    common = owners & me
    parity = jnp.zeros_like(common)
    for at in range(bits):
        parity = parity ^ ((common >> at) & 1)
    index = sample_rows - owners * height + parity * height
    block = min(1024, height)
    sign_bits = sign_bits.reshape(height // block, block // INNER, INNER)
    spot = jnp.stack([me, column // near, column % near]).astype(jnp.int32)

    def halve(keep, send, at):
        got = lax.ppermute(send, "rows", [(r, r ^ (1 << at)) for r in range(groups)])
        half = keep.shape[0] // 2
        if at == bits - 1:
            return keep, got
        return keep[:half] + got[:half], keep[half:] + got[half:]

    def onward(r, c):
        to = c + near if r % 2 == 0 else c - near
        return (r, to) if 0 <= to < columns else (r ^ 1, c)

    def pairs(to):
        ends = [(r, c, *to(r, c)) for r in range(groups) for c in range(columns)]
        return [(r * columns + c, r_to * columns + c_to) for r, c, r_to, c_to in ends]

    ring = pairs(onward)
    mirror = pairs(lambda r, c: (c // near, r * near + c % near))

    plane = [[] for _ in range(near)]
    remote = []
    for strip in range(strips):
        keep, send = picked_strip(slab, sign_bits, index, spot, groups, strip)
        for at in range(bits):
            keep, send = halve(keep, send, at)
            if at == 0:
                index, send = lax.optimization_barrier((index, send))
        own = keep + send
        moving, passed = own, []
        for away in range(1, groups):
            moving = lax.ppermute(moving, AXES, ring)
            passed.append(moving)
        remote.append(passed)
        plane[0].append(own)
        for off in range(1, near):
            plane[off].append(lax.ppermute(own, "cols", [(c, c ^ off) for c in range(columns)]))

    parts = [part for side in plane for part in side]
    depth = samples // groups
    turned = jax.ShapeDtypeStruct((near * width, depth), jnp.bfloat16)
    high, low, own_sums = pl.pallas_call(
        functools.partial(turn_plane, near, strips),
        out_shape=(turned, turned, jax.ShapeDtypeStruct((near * width, width), jnp.float32)),
        in_specs=[SMEM] + [VMEM] * len(parts),
        out_specs=(VMEM,) * 3,
        compiler_params=pltpu.CompilerParams(vmem_limit_bytes=32 * MIB),
        name="turn_plane",
    )(spot, *parts)

    half_sums = jax.ShapeDtypeStruct((groups // 2, near * width, LANES), jnp.float32)
    totals, directs, sideways = [], [], [[] for _ in range(1, near)]
    for strip in range(strips):
        keep, send = pl.pallas_call(
            functools.partial(pair_products, groups, strip),
            out_shape=(half_sums, half_sums),
            in_specs=[SMEM] + [VMEM] * (3 + len(remote[strip])),
            out_specs=(VMEM, VMEM),
            compiler_params=pltpu.CompilerParams(vmem_limit_bytes=32 * MIB),
            name="pair_products",
        )(spot, high, low, own_sums, *remote[strip])
        for at in range(bits):
            keep, send = halve(keep, send, at)
        total = (keep + send)[0]
        totals.append(total)
        directs.append(lax.ppermute(total, AXES, mirror))
        for off in range(1, near):
            part = lax.dynamic_slice_in_dim(total, (column % near ^ off) * width, width, 0)
            sideways[off - 1].append(lax.ppermute(part, "cols", [(c, c ^ off) for c in range(columns)]))

    last = totals + directs + [part for side in sideways for part in side]
    return pl.pallas_call(
        functools.partial(finish, factor, near, strips),
        out_shape=jax.ShapeDtypeStruct((near * width, width), jnp.float32),
        in_specs=[SMEM] + [VMEM] * len(last),
        out_specs=VMEM,
        compiler_params=pltpu.CompilerParams(vmem_limit_bytes=16 * MIB),
        name="finish",
    )(spot, *last)


def solution(mesh):
    return jax.shard_map(
        shards,
        mesh=mesh,
        in_specs=(P("rows", "cols"), P("rows"), P()),
        out_specs=P("rows", "cols"),
        check_vma=False,
    )
```

```python
import functools

import jax
import jax.numpy as jnp
from jax import lax
from jax.experimental import pallas as pl
from jax.experimental.pallas import tpu as pltpu
from jax.sharding import PartitionSpec as P

LANES = 128
INNER = 128
AXES = ("rows", "cols")


def bit_reverse(value, bits):
    return sum(((value >> at) & 1) << (bits - 1 - at) for at in range(bits))


def butterflies(parts):
    stride = 1
    while stride < len(parts):
        for at in range(len(parts)):
            if not at & stride:
                low, high = parts[at], parts[at + stride]
                parts[at], parts[at + stride] = low + high, low - high
        stride *= 2
    return parts


def transform_and_pick(groups, strip, spot_ref, index_ref, bits_ref, slab_ref, keep_ref, send_ref, mixed):
    height = slab_ref.shape[0]
    steps, inner_blocks = bits_ref.shape[0], bits_ref.shape[1]
    block = height // steps
    columns = slice(strip * LANES, (strip + 1) * LANES)

    row = lax.broadcasted_iota(jnp.int32, (INNER, 2 * INNER), 0)
    col = lax.broadcasted_iota(jnp.int32, (INNER, 2 * INNER), 1) & (INNER - 1)
    common = row & col
    for shift in (4, 2, 1):
        common = common ^ (common >> shift)
    table = (1 - 2 * (common & 1)).astype(jnp.float32)

    def combine(starts, negate):
        parts = butterflies([mixed[pl.ds(pl.multiple_of(s, 8), 8), :] for s in starts])
        for s, part in zip(starts, parts):
            mixed[pl.ds(pl.multiple_of(s, 8), 8), :] = part
            if negate:
                mixed[pl.ds(pl.multiple_of(s + height, 8), 8), :] = -part

    @pl.loop(0, steps)
    def _(step):
        base = step * block
        flips = (1 - 2 * bits_ref[step]).astype(jnp.float32)
        for at in range(inner_blocks):
            rows = pl.ds(pl.multiple_of(base + at * INNER, INNER), INNER)
            flip = flips[at : at + 1, :]
            signed = (table * jnp.concatenate([flip, flip], axis=1)).astype(jnp.bfloat16)
            mixed[rows, :] = jnp.dot(
                signed, jnp.concatenate(two_parts(slab_ref[rows, columns]), axis=0), preferred_element_type=jnp.float32
            )

        @pl.loop(0, INNER // 8, unroll=4)
        def _(tile):
            combine([base + at * INNER + tile * 8 for at in range(inner_blocks)], False)

    @pl.loop(0, block // 8, unroll=4)
    def _(tile):
        combine([at * block + tile * 8 for at in range(steps)], True)

    count = index_ref.shape[0] // groups
    bits = groups.bit_length() - 1
    half = groups // 2
    unroll = min(128, count)
    for place in range(groups):
        out = keep_ref if place < half else send_ref
        start = (spot_ref[0] ^ bit_reverse(place, bits)) * count
        to = (place % half) * count

        @pl.loop(0, count // unroll)
        def _(chunk):
            for at in range(unroll):
                source = index_ref[start + chunk * unroll + at]
                out[pl.ds(to + chunk * unroll + at, 1), :] = mixed[pl.ds(source, 1), :]


VMEM = pl.BlockSpec(memory_space=pltpu.VMEM)
SMEM = pl.BlockSpec(memory_space=pltpu.SMEM)
MIB = 1024 * 1024


def picked_strip(slab, sign_bits, index, spot, groups, strip):
    height = slab.shape[0]
    samples = index.shape[0]
    half = jax.ShapeDtypeStruct((samples // 2, LANES), jnp.float32)
    return pl.pallas_call(
        functools.partial(transform_and_pick, groups, strip),
        out_shape=(half, half),
        in_specs=[SMEM, SMEM, VMEM, VMEM],
        out_specs=(VMEM, VMEM),
        scratch_shapes=[pltpu.VMEM((2 * height, LANES), jnp.float32)],
        compiler_params=pltpu.CompilerParams(vmem_limit_bytes=32 * MIB),
        cost_estimate=pl.CostEstimate(
            flops=16 * height * INNER * LANES, bytes_accessed=16 * LANES * (height + samples), transcendentals=0
        ),
        name="transform_and_pick",
    )(spot, index, sign_bits, slab)


def two_parts(values):
    high = values.astype(jnp.bfloat16)
    return high, (values - high.astype(jnp.float32)).astype(jnp.bfloat16)


def three_products(left, right):
    dot = functools.partial(jnp.dot, preferred_element_type=jnp.float32)
    return dot(left[0], right[0]) + dot(left[0], right[1]) + dot(left[1], right[0])


def turn_plane(near, strips, spot_ref, *refs):
    parts, (high_ref, low_ref, own_ref) = refs[:-3], refs[-3:]
    width = own_ref.shape[1]
    for off in range(near):
        for strip in range(strips):
            high, low = two_parts(parts[off * strips + strip][...].T)
            where = pl.ds(pl.multiple_of((spot_ref[2] ^ off) * width + strip * LANES, LANES), LANES)
            high_ref[where, :] = high
            low_ref[where, :] = low
    own = jnp.concatenate([part[...] for part in parts[:strips]], axis=1)
    own_ref[...] = three_products((high_ref[...], low_ref[...]), two_parts(own))


def pair_products(groups, strip, spot_ref, high_ref, low_ref, own_ref, *refs):
    remote, (keep_ref, send_ref) = refs[:-2], refs[-2:]
    me, at_plane = spot_ref[0], spot_ref[1]
    half = keep_ref.shape[0]
    bits = groups.bit_length() - 1
    back = 1 - 2 * (me & 1)

    def store(other, value):
        place = bit_reverse(other ^ me, bits)

        @pl.when(place < half)
        def _():
            keep_ref[place] = value()

        @pl.when(place >= half)
        def _():
            send_ref[place - half] = value()

    store(at_plane, lambda: own_ref[:, strip * LANES : (strip + 1) * LANES])
    for away in range(1, groups):
        below, above = at_plane - away * back, at_plane + away * back

        @pl.when((below >= 0) & (below < groups))
        def _():
            product = three_products((high_ref[...], low_ref[...]), two_parts(remote[away - 1][...]))
            store(below, lambda: product)

        @pl.when((above >= 0) & (above < groups))
        def _():
            store(above, lambda: jnp.zeros(keep_ref.shape[1:], jnp.float32))


def finish(factor, near, strips, spot_ref, *refs):
    totals, directs, turned, out_ref = refs[:strips], refs[strips : 2 * strips], refs[2 * strips : -1], refs[-1]
    me, at_plane, at_near = spot_ref[0], spot_ref[1], spot_ref[2]
    width = out_ref.shape[1]

    @pl.when(me == at_plane)
    def _():
        for strip in range(strips):
            out_ref[:, strip * LANES : (strip + 1) * LANES] = totals[strip][...] * factor

    @pl.when(me != at_plane)
    def _():
        direct = jnp.concatenate([part[...] for part in directs], axis=1) * factor
        out_ref[...] = direct
        for off in range(near):
            start = pl.multiple_of((at_near ^ off) * width, width)
            for strip in range(strips):
                part = totals[strip][pl.ds(start, width), :] if off == 0 else turned[(off - 1) * strips + strip][...]
                rows = pl.ds(pl.multiple_of(start + strip * LANES, LANES), LANES)
                out_ref[rows, :] = out_ref[rows, :] + part.T * factor


def shards(slab, sign_bits, sample_rows):
    height, width = slab.shape
    groups, columns = lax.axis_size("rows"), lax.axis_size("cols")
    near = columns // groups
    strips = width // LANES
    me, column = lax.axis_index("rows"), lax.axis_index("cols")
    samples = sample_rows.shape[0]
    factor = 1.0 / (samples * height * groups)
    bits = groups.bit_length() - 1

    owners = sample_rows // height
    common = owners & me
    parity = jnp.zeros_like(common)
    for at in range(bits):
        parity = parity ^ ((common >> at) & 1)
    index = sample_rows - owners * height + parity * height
    block = min(1024, height)
    sign_bits = sign_bits.reshape(height // block, block // INNER, INNER)
    spot = jnp.stack([me, column // near, column % near]).astype(jnp.int32)

    def halve(keep, send, at):
        got = lax.ppermute(send, "rows", [(r, r ^ (1 << at)) for r in range(groups)])
        half = keep.shape[0] // 2
        if at == bits - 1:
            return keep, got
        return keep[:half] + got[:half], keep[half:] + got[half:]

    def after(value, earlier):
        return lax.optimization_barrier((value, earlier))

    def onward(r, c):
        to = c + near if r % 2 == 0 else c - near
        return (r, to) if 0 <= to < columns else (r ^ 1, c)

    def pairs(to):
        ends = [(r, c, *to(r, c)) for r in range(groups) for c in range(columns)]
        return [(r * columns + c, r_to * columns + c_to) for r, c, r_to, c_to in ends]

    ring = pairs(onward)
    mirror = pairs(lambda r, c: (c // near, r * near + c % near))

    plane = [[] for _ in range(near)]
    remote = []
    for strip in range(strips):
        keep, send = picked_strip(slab, sign_bits, index, spot, groups, strip)
        if strip:
            send, plane[0][-1] = after(send, plane[0][-1])
        for at in range(bits):
            keep, send = halve(keep, send, at)
            if at == 0:
                index, send = after(index, send)
        if strip:
            send, remote[-1][0] = after(send, remote[-1][0])
            for side in plane[1:]:
                send, side[-1] = after(send, side[-1])
        own = keep + send
        moving, passed = own, []
        for away in range(1, groups):
            if strip and away > 1:
                moving, remote[-1][away - 1] = after(moving, remote[-1][away - 1])
            moving = lax.ppermute(moving, AXES, ring)
            passed.append(moving)
        remote.append(passed)
        plane[0].append(own)
        for off in range(1, near):
            plane[off].append(lax.ppermute(own, "cols", [(c, c ^ off) for c in range(columns)]))

    parts = [part for side in plane for part in side]
    depth = samples // groups
    turned = jax.ShapeDtypeStruct((near * width, depth), jnp.bfloat16)
    high, low, own_sums = pl.pallas_call(
        functools.partial(turn_plane, near, strips),
        out_shape=(turned, turned, jax.ShapeDtypeStruct((near * width, width), jnp.float32)),
        in_specs=[SMEM] + [VMEM] * len(parts),
        out_specs=(VMEM,) * 3,
        compiler_params=pltpu.CompilerParams(vmem_limit_bytes=32 * MIB),
        name="turn_plane",
    )(spot, *parts)

    half_sums = jax.ShapeDtypeStruct((groups // 2, near * width, LANES), jnp.float32)
    totals, directs, sideways = [], [], [[] for _ in range(1, near)]
    for strip in range(strips):
        if strip:
            remote[strip][-1], totals[-1] = after(remote[strip][-1], totals[-1])
        keep, send = pl.pallas_call(
            functools.partial(pair_products, groups, strip),
            out_shape=(half_sums, half_sums),
            in_specs=[SMEM] + [VMEM] * (3 + len(remote[strip])),
            out_specs=(VMEM, VMEM),
            compiler_params=pltpu.CompilerParams(vmem_limit_bytes=32 * MIB),
            name="pair_products",
        )(spot, high, low, own_sums, *remote[strip])
        for at in range(bits):
            keep, send = halve(keep, send, at)
        total = (keep + send)[0]
        totals.append(total)
        directs.append(lax.ppermute(total, AXES, mirror))
        for off in range(1, near):
            part = lax.dynamic_slice_in_dim(total, (column % near ^ off) * width, width, 0)
            sideways[off - 1].append(lax.ppermute(part, "cols", [(c, c ^ off) for c in range(columns)]))

    last = totals + directs + [part for side in sideways for part in side]
    return pl.pallas_call(
        functools.partial(finish, factor, near, strips),
        out_shape=jax.ShapeDtypeStruct((near * width, width), jnp.float32),
        in_specs=[SMEM] + [VMEM] * len(last),
        out_specs=VMEM,
        compiler_params=pltpu.CompilerParams(vmem_limit_bytes=16 * MIB),
        name="finish",
    )(spot, *last)


def solution(mesh):
    return jax.shard_map(
        shards,
        mesh=mesh,
        in_specs=(P("rows", "cols"), P("rows"), P()),
        out_specs=P("rows", "cols"),
        check_vma=False,
    )
```

```python
import functools

import jax
import jax.numpy as jnp
from jax import lax
from jax.experimental import pallas as pl
from jax.experimental.pallas import tpu as pltpu
from jax.sharding import PartitionSpec as P

LANES = 128
INNER = 128
AXES = ("rows", "cols")


def bit_reverse(value, bits):
    return sum(((value >> at) & 1) << (bits - 1 - at) for at in range(bits))


def butterflies(parts):
    stride = 1
    while stride < len(parts):
        for at in range(len(parts)):
            if not at & stride:
                low, high = parts[at], parts[at + stride]
                parts[at], parts[at + stride] = low + high, low - high
        stride *= 2
    return parts


def transform_and_pick(groups, strip, spot_ref, index_ref, bits_ref, slab_ref, keep_ref, send_ref, mixed):
    height = slab_ref.shape[0]
    steps, inner_blocks = bits_ref.shape[0], bits_ref.shape[1]
    block = height // steps
    columns = slice(strip * LANES, (strip + 1) * LANES)

    row = lax.broadcasted_iota(jnp.int32, (INNER, 2 * INNER), 0)
    col = lax.broadcasted_iota(jnp.int32, (INNER, 2 * INNER), 1) & (INNER - 1)
    common = row & col
    for shift in (4, 2, 1):
        common = common ^ (common >> shift)
    table = (1 - 2 * (common & 1)).astype(jnp.float32)

    def combine(starts, negate):
        parts = butterflies([mixed[pl.ds(pl.multiple_of(s, 8), 8), :] for s in starts])
        for s, part in zip(starts, parts):
            mixed[pl.ds(pl.multiple_of(s, 8), 8), :] = part
            if negate:
                mixed[pl.ds(pl.multiple_of(s + height, 8), 8), :] = -part

    @pl.loop(0, steps)
    def _(step):
        base = step * block
        flips = (1 - 2 * bits_ref[step]).astype(jnp.float32)
        for at in range(inner_blocks):
            rows = pl.ds(pl.multiple_of(base + at * INNER, INNER), INNER)
            flip = flips[at : at + 1, :]
            signed = (table * jnp.concatenate([flip, flip], axis=1)).astype(jnp.bfloat16)
            mixed[rows, :] = jnp.dot(
                signed, jnp.concatenate(two_parts(slab_ref[rows, columns]), axis=0), preferred_element_type=jnp.float32
            )

        @pl.loop(0, INNER // 8, unroll=4)
        def _(tile):
            combine([base + at * INNER + tile * 8 for at in range(inner_blocks)], False)

    @pl.loop(0, block // 8, unroll=4)
    def _(tile):
        combine([at * block + tile * 8 for at in range(steps)], True)

    count = index_ref.shape[0] // groups
    bits = groups.bit_length() - 1
    half = groups // 2
    unroll = min(128, count)
    for place in range(groups):
        out = keep_ref if place < half else send_ref
        start = (spot_ref[0] ^ bit_reverse(place, bits)) * count
        to = (place % half) * count

        @pl.loop(0, count // unroll)
        def _(chunk):
            for at in range(unroll):
                source = index_ref[start + chunk * unroll + at]
                out[pl.ds(to + chunk * unroll + at, 1), :] = mixed[pl.ds(source, 1), :]


VMEM = pl.BlockSpec(memory_space=pltpu.VMEM)
SMEM = pl.BlockSpec(memory_space=pltpu.SMEM)
MIB = 1024 * 1024


def picked_strip(slab, sign_bits, index, spot, groups, strip):
    height = slab.shape[0]
    samples = index.shape[0]
    half = jax.ShapeDtypeStruct((samples // 2, LANES), jnp.float32)
    return pl.pallas_call(
        functools.partial(transform_and_pick, groups, strip),
        out_shape=(half, half),
        in_specs=[SMEM, SMEM, VMEM, VMEM],
        out_specs=(VMEM, VMEM),
        scratch_shapes=[pltpu.VMEM((2 * height, LANES), jnp.float32)],
        compiler_params=pltpu.CompilerParams(vmem_limit_bytes=32 * MIB),
        cost_estimate=pl.CostEstimate(
            flops=16 * height * INNER * LANES, bytes_accessed=16 * LANES * (height + samples), transcendentals=0
        ),
        name="transform_and_pick",
    )(spot, index, sign_bits, slab)


def two_parts(values):
    high = values.astype(jnp.bfloat16)
    return high, (values - high.astype(jnp.float32)).astype(jnp.bfloat16)


def three_products(left, right):
    dot = functools.partial(jnp.dot, preferred_element_type=jnp.float32)
    return dot(left[0], right[0]) + dot(left[0], right[1]) + dot(left[1], right[0])


def turn_plane(near, strips, spot_ref, *refs):
    parts, (high_ref, low_ref, own_ref) = refs[:-3], refs[-3:]
    width = own_ref.shape[1]
    for off in range(near):
        for strip in range(strips):
            high, low = two_parts(parts[off * strips + strip][...].T)
            where = pl.ds(pl.multiple_of((spot_ref[2] ^ off) * width + strip * LANES, LANES), LANES)
            high_ref[where, :] = high
            low_ref[where, :] = low
    own = jnp.concatenate([part[...] for part in parts[:strips]], axis=1)
    own_ref[...] = three_products((high_ref[...], low_ref[...]), two_parts(own))


def pair_products(groups, strip, flip, spot_ref, high_ref, low_ref, own_ref, *refs):
    remote, (keep_ref, send_ref) = refs[:-2], refs[-2:]
    me, at_plane = spot_ref[0], spot_ref[1]
    half = keep_ref.shape[0]
    bits = groups.bit_length() - 1
    back = 1 - 2 * (me & 1)

    def store(other, value):
        place = bit_reverse(other ^ me ^ flip, bits)

        @pl.when(place < half)
        def _():
            keep_ref[place] = value()

        @pl.when(place >= half)
        def _():
            send_ref[place - half] = value()

    store(at_plane, lambda: own_ref[:, strip * LANES : (strip + 1) * LANES])
    for away in range(1, groups):
        below, above = at_plane - away * back, at_plane + away * back

        @pl.when((below >= 0) & (below < groups))
        def _():
            product = three_products((high_ref[...], low_ref[...]), two_parts(remote[away - 1][...]))
            store(below, lambda: product)

        @pl.when((above >= 0) & (above < groups))
        def _():
            store(above, lambda: jnp.zeros(keep_ref.shape[1:], jnp.float32))


def finish(factor, strips, spot_ref, *refs):
    directs, turned, out_ref = refs[:strips], refs[strips:-1], refs[-1]
    width = out_ref.shape[1]
    for at, part in enumerate(turned):
        start = (spot_ref[2] ^ (at // strips)) * width + at % strips * LANES
        out_ref[pl.ds(pl.multiple_of(start, LANES), LANES), :] = part[...].T * factor

    @pl.when(spot_ref[0] != spot_ref[1])
    def _():
        direct = jnp.concatenate([part[...] for part in directs], axis=1)
        out_ref[...] = out_ref[...] + direct * factor


def shards(slab, sign_bits, sample_rows):
    height, width = slab.shape
    groups, columns = lax.axis_size("rows"), lax.axis_size("cols")
    near = columns // groups
    strips = width // LANES
    me, column = lax.axis_index("rows"), lax.axis_index("cols")
    samples = sample_rows.shape[0]
    factor = 1.0 / (samples * height * groups)
    bits = groups.bit_length() - 1

    owners = sample_rows // height
    common = owners & me
    parity = jnp.zeros_like(common)
    for at in range(bits):
        parity = parity ^ ((common >> at) & 1)
    index = sample_rows - owners * height + parity * height
    block = min(1024, height)
    sign_bits = sign_bits.reshape(height // block, block // INNER, INNER)
    spot = jnp.stack([me, column // near, column % near]).astype(jnp.int32)

    def halve(keep, send, at):
        got = lax.ppermute(send, "rows", [(r, r ^ (1 << at)) for r in range(groups)])
        half = keep.shape[0] // 2
        if at == bits - 1:
            return keep, got
        return keep[:half] + got[:half], keep[half:] + got[half:]

    def after(value, earlier):
        return lax.optimization_barrier((value, earlier))

    def onward(r, c):
        to = c + near if r % 2 == 0 else c - near
        return (r, to) if 0 <= to < columns else (r ^ 1, c)

    def pairs(to):
        ends = [(r, c, *to(r, c)) for r in range(groups) for c in range(columns)]
        return [(r * columns + c, r_to * columns + c_to) for r, c, r_to, c_to in ends]

    ring = pairs(onward)

    plane = [[] for _ in range(near)]
    remote = []
    for strip in range(strips):
        keep, send = picked_strip(slab, sign_bits, index, spot, groups, strip)
        if strip:
            send, plane[0][-1] = after(send, plane[0][-1])
        for at in range(bits):
            keep, send = halve(keep, send, at)
            if at == 0:
                index, send = after(index, send)
        if strip:
            send, remote[-1][0] = after(send, remote[-1][0])
            for side in plane[1:]:
                send, side[-1] = after(send, side[-1])
        own = keep + send
        moving, passed = own, []
        for away in range(1, groups):
            if strip and away > 1:
                moving, remote[-1][away - 1] = after(moving, remote[-1][away - 1])
            moving = lax.ppermute(moving, AXES, ring)
            passed.append(moving)
        remote.append(passed)
        plane[0].append(own)
        for off in range(1, near):
            plane[off].append(lax.ppermute(own, "cols", [(c, c ^ off) for c in range(columns)]))

    parts = [part for side in plane for part in side]
    depth = samples // groups
    turned = jax.ShapeDtypeStruct((near * width, depth), jnp.bfloat16)
    high, low, own_sums = pl.pallas_call(
        functools.partial(turn_plane, near, strips),
        out_shape=(turned, turned, jax.ShapeDtypeStruct((near * width, width), jnp.float32)),
        in_specs=[SMEM] + [VMEM] * len(parts),
        out_specs=(VMEM,) * 3,
        compiler_params=pltpu.CompilerParams(vmem_limit_bytes=32 * MIB),
        name="turn_plane",
    )(spot, *parts)

    half_sums = jax.ShapeDtypeStruct((groups // 2, near * width, LANES), jnp.float32)
    totals, directs, sideways = [], [], [[] for _ in range(near)]
    for strip in range(strips):
        flip = strip % 2 * (groups // 2)
        keep, send = pl.pallas_call(
            functools.partial(pair_products, groups, strip, flip),
            out_shape=(half_sums, half_sums),
            in_specs=[SMEM] + [VMEM] * (3 + len(remote[strip])),
            out_specs=(VMEM, VMEM),
            compiler_params=pltpu.CompilerParams(vmem_limit_bytes=32 * MIB),
            name="pair_products",
        )(spot, high, low, own_sums, *remote[strip])
        if strip:
            send, totals[-1] = after(send, totals[-1])
        for at in range(bits):
            keep, send = halve(keep, send, at)
        total = (keep + send)[0]
        totals.append(total)
        directs.append(lax.ppermute(total, AXES, pairs(lambda r, c: (c // near, (r ^ flip) * near + c % near))))
        for off in range(near):
            part = lax.dynamic_slice_in_dim(total, (column % near ^ off) * width, width, 0)
            if off or flip:
                part = lax.ppermute(part, AXES, pairs(lambda r, c: (r ^ flip, c ^ off)))
            sideways[off].append(part)

    last = directs + [part for side in sideways for part in side]
    return pl.pallas_call(
        functools.partial(finish, factor, strips),
        out_shape=jax.ShapeDtypeStruct((near * width, width), jnp.float32),
        in_specs=[SMEM] + [VMEM] * len(last),
        out_specs=VMEM,
        compiler_params=pltpu.CompilerParams(vmem_limit_bytes=16 * MIB),
        name="finish",
    )(spot, *last)


def solution(mesh):
    return jax.shard_map(
        shards,
        mesh=mesh,
        in_specs=(P("rows", "cols"), P("rows"), P()),
        out_specs=P("rows", "cols"),
        check_vma=False,
    )
```

```python
import functools

import jax
import jax.numpy as jnp
from jax import lax
from jax.experimental import pallas as pl
from jax.experimental.pallas import tpu as pltpu
from jax.sharding import PartitionSpec as P

LANES = 128
INNER = 128
AXES = ("rows", "cols")


def bit_reverse(value, bits):
    return sum(((value >> at) & 1) << (bits - 1 - at) for at in range(bits))


def butterflies(parts):
    stride = 1
    while stride < len(parts):
        for at in range(len(parts)):
            if not at & stride:
                low, high = parts[at], parts[at + stride]
                parts[at], parts[at + stride] = low + high, low - high
        stride *= 2
    return parts


def transform_and_pick(groups, strip, spot_ref, index_ref, bits_ref, slab_ref, keep_ref, send_ref, mixed):
    height = slab_ref.shape[0]
    steps, inner_blocks = bits_ref.shape[0], bits_ref.shape[1]
    block = height // steps
    columns = slice(strip * LANES, (strip + 1) * LANES)

    row = lax.broadcasted_iota(jnp.int32, (INNER, 2 * INNER), 0)
    col = lax.broadcasted_iota(jnp.int32, (INNER, 2 * INNER), 1) & (INNER - 1)
    common = row & col
    for shift in (4, 2, 1):
        common = common ^ (common >> shift)
    table = (1 - 2 * (common & 1)).astype(jnp.float32)

    def combine(starts, negate):
        parts = butterflies([mixed[pl.ds(pl.multiple_of(s, 8), 8), :] for s in starts])
        for s, part in zip(starts, parts):
            mixed[pl.ds(pl.multiple_of(s, 8), 8), :] = part
            if negate:
                mixed[pl.ds(pl.multiple_of(s + height, 8), 8), :] = -part

    @pl.loop(0, steps)
    def _(step):
        base = step * block
        flips = (1 - 2 * bits_ref[step]).astype(jnp.float32)
        for at in range(inner_blocks):
            rows = pl.ds(pl.multiple_of(base + at * INNER, INNER), INNER)
            flip = flips[at : at + 1, :]
            signed = (table * jnp.concatenate([flip, flip], axis=1)).astype(jnp.bfloat16)
            mixed[rows, :] = jnp.dot(
                signed, jnp.concatenate(two_parts(slab_ref[rows, columns]), axis=0), preferred_element_type=jnp.float32
            )

        @pl.loop(0, INNER // 8, unroll=4)
        def _(tile):
            combine([base + at * INNER + tile * 8 for at in range(inner_blocks)], False)

    @pl.loop(0, block // 8, unroll=4)
    def _(tile):
        combine([at * block + tile * 8 for at in range(steps)], True)

    gather(groups, groups // 2, spot_ref, index_ref, mixed, send_ref)
    if keep_ref is not None:
        gather(groups, 0, spot_ref, index_ref, mixed, keep_ref)


def gather(groups, first, spot_ref, index_ref, mixed, out_ref):
    count = index_ref.shape[0] // groups
    bits = groups.bit_length() - 1
    unroll = min(128, count)
    for place in range(groups // 2):
        start = (spot_ref[0] ^ bit_reverse(first + place, bits)) * count

        @pl.loop(0, count // unroll)
        def _(chunk):
            for at in range(unroll):
                source = index_ref[start + chunk * unroll + at]
                out_ref[pl.ds(place * count + chunk * unroll + at, 1), :] = mixed[pl.ds(source, 1), :]


VMEM = pl.BlockSpec(memory_space=pltpu.VMEM)
SMEM = pl.BlockSpec(memory_space=pltpu.SMEM)
MIB = 1024 * 1024


def picked_strip(slab, sign_bits, index, spot, groups, strip):
    height = slab.shape[0]
    samples = index.shape[0]
    half = jax.ShapeDtypeStruct((samples // 2, LANES), jnp.float32)
    table = jax.ShapeDtypeStruct((2 * height, LANES), jnp.float32)
    transform = functools.partial(transform_and_pick, groups, strip)
    if strip:
        kernel, out_shape, scratch = transform, (half, half), [pltpu.VMEM(table.shape, table.dtype)]
    else:
        kernel, out_shape, scratch = lambda *refs: transform(*refs[:4], None, *refs[4:]), (half, table), []
    first, second = pl.pallas_call(
        kernel,
        out_shape=out_shape,
        in_specs=[SMEM, SMEM, VMEM, VMEM],
        out_specs=(VMEM, VMEM),
        scratch_shapes=scratch,
        compiler_params=pltpu.CompilerParams(vmem_limit_bytes=32 * MIB),
        cost_estimate=pl.CostEstimate(
            flops=16 * height * INNER * LANES, bytes_accessed=16 * LANES * (height + samples), transcendentals=0
        ),
        name="transform_and_pick",
    )(spot, index, sign_bits, slab)
    if strip:
        return first, second
    keep = pl.pallas_call(
        functools.partial(gather, groups, 0),
        out_shape=half,
        in_specs=[SMEM, SMEM, VMEM],
        out_specs=VMEM,
        compiler_params=pltpu.CompilerParams(vmem_limit_bytes=32 * MIB),
        name="pick",
    )(spot, index, second)
    return keep, first


def two_parts(values):
    high = values.astype(jnp.bfloat16)
    return high, (values - high.astype(jnp.float32)).astype(jnp.bfloat16)


def three_products(left, right):
    dot = functools.partial(jnp.dot, preferred_element_type=jnp.float32)
    width = right[0].shape[1]
    both = dot(left[0], jnp.concatenate(right, axis=1))
    return both[:, :width] + both[:, width:] + dot(left[1], right[0])


def turn_plane(near, strips, spot_ref, *refs):
    parts, (high_ref, low_ref, own_ref) = refs[:-3], refs[-3:]
    width = own_ref.shape[1]
    for off in range(near):
        for strip in range(strips):
            high, low = two_parts(parts[off * strips + strip][...].T)
            where = pl.ds(pl.multiple_of((spot_ref[2] ^ off) * width + strip * LANES, LANES), LANES)
            high_ref[where, :] = high
            low_ref[where, :] = low
    own = jnp.concatenate([part[...] for part in parts[:strips]], axis=1)
    own_ref[...] = three_products((high_ref[...], low_ref[...]), two_parts(own))


def pair_products(groups, strip, flip, spot_ref, high_ref, low_ref, own_ref, *refs):
    remote, (keep_ref, send_ref) = refs[:-2], refs[-2:]
    me, at_plane = spot_ref[0], spot_ref[1]
    half = keep_ref.shape[0]
    bits = groups.bit_length() - 1
    back = 1 - 2 * (me & 1)

    def store(other, value):
        place = bit_reverse(other ^ me ^ flip, bits)

        @pl.when(place < half)
        def _():
            keep_ref[place] = value()

        @pl.when(place >= half)
        def _():
            send_ref[place - half] = value()

    store(at_plane, lambda: own_ref[:, strip * LANES : (strip + 1) * LANES])
    for away in range(1, groups):
        below, above = at_plane - away * back, at_plane + away * back

        @pl.when((below >= 0) & (below < groups))
        def _():
            product = three_products((high_ref[...], low_ref[...]), two_parts(remote[away - 1][...]))
            store(below, lambda: product)

        @pl.when((above >= 0) & (above < groups))
        def _():
            store(above, lambda: jnp.zeros(keep_ref.shape[1:], jnp.float32))


def finish(factor, strips, spot_ref, *refs):
    directs, turned, out_ref = refs[:strips], refs[strips:-1], refs[-1]
    width = out_ref.shape[1]
    for at, part in enumerate(turned):
        start = (spot_ref[2] ^ (at // strips)) * width + at % strips * LANES
        out_ref[pl.ds(pl.multiple_of(start, LANES), LANES), :] = part[...].T * factor

    @pl.when(spot_ref[0] != spot_ref[1])
    def _():
        direct = jnp.concatenate([part[...] for part in directs], axis=1)
        out_ref[...] = out_ref[...] + direct * factor


def shards(slab, sign_bits, sample_rows):
    height, width = slab.shape
    groups, columns = lax.axis_size("rows"), lax.axis_size("cols")
    near = columns // groups
    strips = width // LANES
    me, column = lax.axis_index("rows"), lax.axis_index("cols")
    samples = sample_rows.shape[0]
    factor = 1.0 / (samples * height * groups)
    bits = groups.bit_length() - 1

    owners = sample_rows // height
    common = owners & me
    parity = jnp.zeros_like(common)
    for at in range(bits):
        parity = parity ^ ((common >> at) & 1)
    index = sample_rows - owners * height + parity * height
    block = min(1024, height)
    sign_bits = sign_bits.reshape(height // block, block // INNER, INNER)
    spot = jnp.stack([me, column // near, column % near]).astype(jnp.int32)

    def halve(keep, send, at):
        got = lax.ppermute(send, "rows", [(r, r ^ (1 << at)) for r in range(groups)])
        half = keep.shape[0] // 2
        if at == bits - 1:
            return keep, got
        return keep[:half] + got[:half], keep[half:] + got[half:]

    def after(value, earlier):
        return lax.optimization_barrier((value, earlier))

    def onward(r, c):
        to = c + near if r % 2 == 0 else c - near
        return (r, to) if 0 <= to < columns else (r ^ 1, c)

    def pairs(to):
        ends = [(r, c, *to(r, c)) for r in range(groups) for c in range(columns)]
        return [(r * columns + c, r_to * columns + c_to) for r, c, r_to, c_to in ends]

    ring = pairs(onward)

    plane = [[] for _ in range(near)]
    remote, onward_parts = [], []
    for strip in range(strips):
        keep, send = picked_strip(slab, sign_bits, index, spot, groups, strip)
        if strip:
            send, plane[0][-1] = after(send, plane[0][-1])
        for at in range(bits):
            keep, send = halve(keep, send, at)
            if at == 0:
                index, send = after(index, send)
        if strip:
            send, remote[-1][0] = after(send, remote[-1][0])
            for side in plane[1:]:
                send, side[-1] = after(send, side[-1])
        own = keep + send
        moving, passed = own, []
        for away in range(1, groups - 1 if strip else groups):
            if strip and away > 1:
                moving, remote[-1][away - 1] = after(moving, remote[-1][away - 1])
            moving = lax.ppermute(moving, AXES, ring)
            passed.append(moving)
        if strip:
            moving, remote[-1][-1] = after(moving, remote[-1][-1])
        onward_parts.append(moving)
        remote.append(passed)
        plane[0].append(own)
        for off in range(1, near):
            plane[off].append(lax.ppermute(own, "cols", [(c, c ^ off) for c in range(columns)]))

    parts = [part for side in plane for part in side]
    depth = samples // groups
    turned = jax.ShapeDtypeStruct((near * width, depth), jnp.bfloat16)
    high, low, own_sums = pl.pallas_call(
        functools.partial(turn_plane, near, strips),
        out_shape=(turned, turned, jax.ShapeDtypeStruct((near * width, width), jnp.float32)),
        in_specs=[SMEM] + [VMEM] * len(parts),
        out_specs=(VMEM,) * 3,
        compiler_params=pltpu.CompilerParams(vmem_limit_bytes=32 * MIB),
        name="turn_plane",
    )(spot, *parts)

    half_sums = jax.ShapeDtypeStruct((groups // 2, near * width, LANES), jnp.float32)
    totals, directs, sideways = [], [], [[] for _ in range(near)]
    for strip in range(strips):
        flip = strip % 2 * (groups // 2)
        keep, send = pl.pallas_call(
            functools.partial(pair_products, groups, strip, flip),
            out_shape=(half_sums, half_sums),
            in_specs=[SMEM] + [VMEM] * (3 + len(remote[strip])),
            out_specs=(VMEM, VMEM),
            compiler_params=pltpu.CompilerParams(vmem_limit_bytes=32 * MIB),
            name="pair_products",
        )(spot, high, low, own_sums, *remote[strip])
        if strip + 1 < strips:
            moving, send = after(onward_parts[strip + 1], send)
            remote[strip + 1].append(lax.ppermute(moving, AXES, ring))
        if strip:
            send, totals[-1] = after(send, totals[-1])
        for at in range(bits):
            keep, send = halve(keep, send, at)
        total = (keep + send)[0]
        totals.append(total)
        directs.append(lax.ppermute(total, AXES, pairs(lambda r, c: (c // near, (r ^ flip) * near + c % near))))
        for off in range(near):
            part = lax.dynamic_slice_in_dim(total, (column % near ^ off) * width, width, 0)
            if off or flip:
                part = lax.ppermute(part, AXES, pairs(lambda r, c: (r ^ flip, c ^ off)))
            sideways[off].append(part)

    last = directs + [part for side in sideways for part in side]
    return pl.pallas_call(
        functools.partial(finish, factor, strips),
        out_shape=jax.ShapeDtypeStruct((near * width, width), jnp.float32),
        in_specs=[SMEM] + [VMEM] * len(last),
        out_specs=VMEM,
        compiler_params=pltpu.CompilerParams(vmem_limit_bytes=16 * MIB),
        name="finish",
    )(spot, *last)


def solution(mesh):
    return jax.shard_map(
        shards,
        mesh=mesh,
        in_specs=(P("rows", "cols"), P("rows"), P()),
        out_specs=P("rows", "cols"),
        check_vma=False,
    )
```

```python
import functools

import jax
import jax.numpy as jnp
from jax import lax
from jax.experimental import pallas as pl
from jax.experimental.pallas import tpu as pltpu
from jax.sharding import PartitionSpec as P

LANES = 128
INNER = 128
AXES = ("rows", "cols")


def bit_reverse(value, bits):
    return sum(((value >> at) & 1) << (bits - 1 - at) for at in range(bits))


def butterflies(parts):
    stride = 1
    while stride < len(parts):
        for at in range(len(parts)):
            if not at & stride:
                low, high = parts[at], parts[at + stride]
                parts[at], parts[at + stride] = low + high, low - high
        stride *= 2
    return parts


def transform_and_pick(groups, strip, spot_ref, index_ref, bits_ref, slab_ref, keep_ref, send_ref, mixed):
    height = slab_ref.shape[0]
    steps, inner_blocks = bits_ref.shape[0], bits_ref.shape[1]
    block = height // steps
    columns = slice(strip * LANES, (strip + 1) * LANES)

    row = lax.broadcasted_iota(jnp.int32, (INNER, 2 * INNER), 0)
    col = lax.broadcasted_iota(jnp.int32, (INNER, 2 * INNER), 1) & (INNER - 1)
    common = row & col
    for shift in (4, 2, 1):
        common = common ^ (common >> shift)
    table = (1 - 2 * (common & 1)).astype(jnp.float32)

    def combine(starts, negate):
        parts = butterflies([mixed[pl.ds(pl.multiple_of(s, 8), 8), :] for s in starts])
        for s, part in zip(starts, parts):
            mixed[pl.ds(pl.multiple_of(s, 8), 8), :] = part
            if negate:
                mixed[pl.ds(pl.multiple_of(s + height, 8), 8), :] = -part

    @pl.loop(0, steps)
    def _(step):
        base = step * block
        flips = (1 - 2 * bits_ref[step]).astype(jnp.float32)
        for at in range(inner_blocks):
            rows = pl.ds(pl.multiple_of(base + at * INNER, INNER), INNER)
            flip = flips[at : at + 1, :]
            signed = (table * jnp.concatenate([flip, flip], axis=1)).astype(jnp.bfloat16)
            mixed[rows, :] = jnp.dot(
                signed, jnp.concatenate(two_parts(slab_ref[rows, columns]), axis=0), preferred_element_type=jnp.float32
            )

        @pl.loop(0, INNER // 8, unroll=4)
        def _(tile):
            combine([base + at * INNER + tile * 8 for at in range(inner_blocks)], False)

    @pl.loop(0, block // 8, unroll=4)
    def _(tile):
        combine([at * block + tile * 8 for at in range(steps)], True)

    gather(groups, groups // 2, spot_ref, index_ref, mixed, send_ref)
    if keep_ref is not None:
        gather(groups, 0, spot_ref, index_ref, mixed, keep_ref)


def gather(groups, first, spot_ref, index_ref, mixed, out_ref):
    count = index_ref.shape[0] // groups
    bits = groups.bit_length() - 1
    unroll = min(128, count)
    for place in range(groups // 2):
        start = (spot_ref[0] ^ bit_reverse(first + place, bits)) * count

        @pl.loop(0, count // unroll)
        def _(chunk):
            for at in range(unroll):
                source = index_ref[start + chunk * unroll + at]
                out_ref[pl.ds(place * count + chunk * unroll + at, 1), :] = mixed[pl.ds(source, 1), :]


VMEM = pl.BlockSpec(memory_space=pltpu.VMEM)
SMEM = pl.BlockSpec(memory_space=pltpu.SMEM)
MIB = 1024 * 1024


def picked_strip(slab, sign_bits, index, spot, groups, strip):
    height = slab.shape[0]
    samples = index.shape[0]
    half = jax.ShapeDtypeStruct((samples // 2, LANES), jnp.float32)
    table = jax.ShapeDtypeStruct((2 * height, LANES), jnp.float32)
    transform = functools.partial(transform_and_pick, groups, strip)
    if strip:
        kernel, out_shape, scratch = transform, (half, half), [pltpu.VMEM(table.shape, table.dtype)]
    else:
        kernel, out_shape, scratch = lambda *refs: transform(*refs[:4], None, *refs[4:]), (half, table), []
    first, second = pl.pallas_call(
        kernel,
        out_shape=out_shape,
        in_specs=[SMEM, SMEM, VMEM, VMEM],
        out_specs=(VMEM, VMEM),
        scratch_shapes=scratch,
        compiler_params=pltpu.CompilerParams(vmem_limit_bytes=32 * MIB),
        cost_estimate=pl.CostEstimate(
            flops=16 * height * INNER * LANES, bytes_accessed=16 * LANES * (height + samples), transcendentals=0
        ),
        name="transform_and_pick",
    )(spot, index, sign_bits, slab)
    if strip:
        return first, second
    keep = pl.pallas_call(
        functools.partial(gather, groups, 0),
        out_shape=half,
        in_specs=[SMEM, SMEM, VMEM],
        out_specs=VMEM,
        compiler_params=pltpu.CompilerParams(vmem_limit_bytes=32 * MIB),
        name="pick",
    )(spot, index, second)
    return keep, first


def two_parts(values):
    high = values.astype(jnp.bfloat16)
    return high, (values - high.astype(jnp.float32)).astype(jnp.bfloat16)


def three_products(left, right):
    dot = functools.partial(jnp.dot, preferred_element_type=jnp.float32)
    width = right[0].shape[1]
    both = dot(left[0], jnp.concatenate(right, axis=1))
    return both[:, :width] + both[:, width:] + dot(left[1], right[0])


def turn_plane(near, strips, spot_ref, *refs):
    parts, (high_ref, low_ref, own_ref) = refs[:-3], refs[-3:]
    width = own_ref.shape[1]
    for off in range(near):
        for strip in range(strips):
            high, low = two_parts(parts[off * strips + strip][...].T)
            where = pl.ds(pl.multiple_of((spot_ref[2] ^ off) * width + strip * LANES, LANES), LANES)
            high_ref[where, :] = high
            low_ref[where, :] = low
    own = jnp.concatenate([part[...] for part in parts[:strips]], axis=1)
    own_ref[...] = three_products((high_ref[...], low_ref[...]), two_parts(own))


def pair_products(groups, strip, flip, spot_ref, high_ref, low_ref, own_ref, *refs):
    remote, (keep_ref, send_ref) = refs[:-2], refs[-2:]
    me, at_plane = spot_ref[0], spot_ref[1]
    half = keep_ref.shape[0]
    bits = groups.bit_length() - 1
    back = 1 - 2 * (me & 1)

    def store(other, value):
        place = bit_reverse(other ^ me ^ flip, bits)

        @pl.when(place < half)
        def _():
            keep_ref[place] = value()

        @pl.when(place >= half)
        def _():
            send_ref[place - half] = value()

    store(at_plane, lambda: own_ref[:, strip * LANES : (strip + 1) * LANES])
    for away in range(1, groups):
        below, above = at_plane - away * back, at_plane + away * back

        @pl.when((below >= 0) & (below < groups))
        def _():
            product = three_products((high_ref[...], low_ref[...]), two_parts(remote[away - 1][...]))
            store(below, lambda: product)

        @pl.when((above >= 0) & (above < groups))
        def _():
            store(above, lambda: jnp.zeros(keep_ref.shape[1:], jnp.float32))


def finish(factor, strips, spot_ref, *refs):
    directs, turned, out_ref = refs[:strips], refs[strips:-1], refs[-1]
    width = out_ref.shape[1]
    for at, part in enumerate(turned):
        start = (spot_ref[2] ^ (at // strips)) * width + at % strips * LANES
        out_ref[pl.ds(pl.multiple_of(start, LANES), LANES), :] = part[...].T * factor

    @pl.when(spot_ref[0] != spot_ref[1])
    def _():
        direct = jnp.concatenate([part[...] for part in directs], axis=1)
        out_ref[...] = out_ref[...] + direct * factor


def shards(slab, sign_bits, sample_rows):
    height, width = slab.shape
    groups, columns = lax.axis_size("rows"), lax.axis_size("cols")
    near = columns // groups
    strips = width // LANES
    me, column = lax.axis_index("rows"), lax.axis_index("cols")
    samples = sample_rows.shape[0]
    factor = 1.0 / (samples * height * groups)
    bits = groups.bit_length() - 1

    owners = sample_rows // height
    common = owners & me
    parity = jnp.zeros_like(common)
    for at in range(bits):
        parity = parity ^ ((common >> at) & 1)
    index = sample_rows - owners * height + parity * height
    block = min(1024, height)
    sign_bits = sign_bits.reshape(height // block, block // INNER, INNER)
    spot = jnp.stack([me, column // near, column % near]).astype(jnp.int32)

    def halve(keep, send, at):
        got = lax.ppermute(send, "rows", [(r, r ^ (1 << at)) for r in range(groups)])
        half = keep.shape[0] // 2
        if at == bits - 1:
            return keep, got
        return keep[:half] + got[:half], keep[half:] + got[half:]

    def after(value, earlier):
        return lax.optimization_barrier((value, earlier))

    def onward(r, c):
        to = c + near if r % 2 == 0 else c - near
        return (r, to) if 0 <= to < columns else (r ^ 1, c)

    def pairs(to):
        ends = [(r, c, *to(r, c)) for r in range(groups) for c in range(columns)]
        return [(r * columns + c, r_to * columns + c_to) for r, c, r_to, c_to in ends]

    ring = pairs(onward)

    plane = [[] for _ in range(near)]
    remote, onward_parts = [], []
    for strip in range(strips):
        keep, send = picked_strip(slab, sign_bits, index, spot, groups, strip)
        if strip:
            send, plane[0][-1] = after(send, plane[0][-1])
        for at in range(bits):
            keep, send = halve(keep, send, at)
            if at == 0:
                index, send = after(index, send)
        if strip:
            send, remote[-1][0] = after(send, remote[-1][0])
            for side in plane[1:]:
                send, side[-1] = after(send, side[-1])
        own = keep + send
        moving, passed = own, []
        for away in range(1, groups - 1 if strip else groups):
            if strip and away > 1:
                moving, remote[-1][away - 1] = after(moving, remote[-1][away - 1])
            moving = lax.ppermute(moving, AXES, ring)
            passed.append(moving)
        if strip:
            moving, remote[-1][-1] = after(moving, remote[-1][-1])
        onward_parts.append(moving)
        remote.append(passed)
        plane[0].append(own)
        for off in range(1, near):
            plane[off].append(lax.ppermute(own, "cols", [(c, c ^ off) for c in range(columns)]))

    parts = [part for side in plane for part in side]
    depth = samples // groups
    turned = jax.ShapeDtypeStruct((near * width, depth), jnp.bfloat16)
    high, low, own_sums = pl.pallas_call(
        functools.partial(turn_plane, near, strips),
        out_shape=(turned, turned, jax.ShapeDtypeStruct((near * width, width), jnp.float32)),
        in_specs=[SMEM] + [VMEM] * len(parts),
        out_specs=(VMEM,) * 3,
        compiler_params=pltpu.CompilerParams(vmem_limit_bytes=32 * MIB),
        name="turn_plane",
    )(spot, *parts)

    half_sums = jax.ShapeDtypeStruct((groups // 2, near * width, LANES), jnp.float32)
    totals, directs, sideways = [], [], [[] for _ in range(near)]
    for strip in range(strips):
        flip = strip % 2 * (groups // 2)
        keep, send = pl.pallas_call(
            functools.partial(pair_products, groups, strip, flip),
            out_shape=(half_sums, half_sums),
            in_specs=[SMEM] + [VMEM] * (3 + len(remote[strip])),
            out_specs=(VMEM, VMEM),
            compiler_params=pltpu.CompilerParams(vmem_limit_bytes=32 * MIB),
            name="pair_products",
        )(spot, high, low, own_sums, *remote[strip])
        if strip + 1 < strips:
            moving, send = after(onward_parts[strip + 1], send)
            remote[strip + 1].append(lax.ppermute(moving, AXES, ring))
        if strip:
            send, totals[-1] = after(send, totals[-1])
        for at in range(bits):
            keep, send = halve(keep, send, at)
        if strip:
            for side in sideways[1:]:
                send, side[-1] = after(send, side[-1])
        total = (keep + send)[0]
        totals.append(total)
        directs.append(lax.ppermute(total, AXES, pairs(lambda r, c: (c // near, (r ^ flip) * near + c % near))))
        for off in range(near):
            part = lax.dynamic_slice_in_dim(total, (column % near ^ off) * width, width, 0)
            if off or flip:
                part = lax.ppermute(part, AXES, pairs(lambda r, c: (r ^ flip, c ^ off)))
            sideways[off].append(part)

    last = directs + [part for side in sideways for part in side]
    return pl.pallas_call(
        functools.partial(finish, factor, strips),
        out_shape=jax.ShapeDtypeStruct((near * width, width), jnp.float32),
        in_specs=[SMEM] + [VMEM] * len(last),
        out_specs=VMEM,
        compiler_params=pltpu.CompilerParams(vmem_limit_bytes=16 * MIB),
        name="finish",
    )(spot, *last)


def solution(mesh):
    return jax.shard_map(
        shards,
        mesh=mesh,
        in_specs=(P("rows", "cols"), P("rows"), P()),
        out_specs=P("rows", "cols"),
        check_vma=False,
    )
```

```python
import functools

import jax
import jax.numpy as jnp
from jax import lax
from jax.experimental import pallas as pl
from jax.experimental.pallas import tpu as pltpu
from jax.sharding import PartitionSpec as P

LANES = 128
INNER = 128
AXES = ("rows", "cols")


def bit_reverse(value, bits):
    return sum(((value >> at) & 1) << (bits - 1 - at) for at in range(bits))


def butterflies(parts):
    stride = 1
    while stride < len(parts):
        for at in range(len(parts)):
            if not at & stride:
                low, high = parts[at], parts[at + stride]
                parts[at], parts[at + stride] = low + high, low - high
        stride *= 2
    return parts


def transform_and_pick(groups, strip, spot_ref, index_ref, bits_ref, slab_ref, keep_ref, send_ref, mixed):
    height = slab_ref.shape[0]
    steps, inner_blocks = bits_ref.shape[0], bits_ref.shape[1]
    block = height // steps
    columns = slice(strip * LANES, (strip + 1) * LANES)

    row = lax.broadcasted_iota(jnp.int32, (INNER, 2 * INNER), 0)
    col = lax.broadcasted_iota(jnp.int32, (INNER, 2 * INNER), 1) & (INNER - 1)
    common = row & col
    for shift in (4, 2, 1):
        common = common ^ (common >> shift)
    table = (1 - 2 * (common & 1)).astype(jnp.float32)

    def combine(starts, negate):
        parts = butterflies([mixed[pl.ds(pl.multiple_of(s, 8), 8), :] for s in starts])
        for s, part in zip(starts, parts):
            mixed[pl.ds(pl.multiple_of(s, 8), 8), :] = part
            if negate:
                mixed[pl.ds(pl.multiple_of(s + height, 8), 8), :] = -part

    @pl.loop(0, steps)
    def _(step):
        base = step * block
        flips = (1 - 2 * bits_ref[step]).astype(jnp.float32)
        for at in range(inner_blocks):
            rows = pl.ds(pl.multiple_of(base + at * INNER, INNER), INNER)
            flip = flips[at : at + 1, :]
            signed = (table * jnp.concatenate([flip, flip], axis=1)).astype(jnp.bfloat16)
            mixed[rows, :] = jnp.dot(
                signed, jnp.concatenate(two_parts(slab_ref[rows, columns]), axis=0), preferred_element_type=jnp.float32
            )

        @pl.loop(0, INNER // 8, unroll=8)
        def _(tile):
            combine([base + at * INNER + tile * 8 for at in range(inner_blocks)], False)

    @pl.loop(0, block // 8, unroll=8)
    def _(tile):
        combine([at * block + tile * 8 for at in range(steps)], True)

    gather(groups, groups // 2, spot_ref, index_ref, mixed, send_ref)
    if keep_ref is not None:
        gather(groups, 0, spot_ref, index_ref, mixed, keep_ref)


def gather(groups, first, spot_ref, index_ref, mixed, out_ref):
    count = index_ref.shape[0] // groups
    bits = groups.bit_length() - 1
    unroll = min(256, count)
    for place in range(groups // 2):
        start = (spot_ref[0] ^ bit_reverse(first + place, bits)) * count

        @pl.loop(0, count // unroll)
        def _(chunk):
            for at in range(unroll):
                source = index_ref[start + chunk * unroll + at]
                out_ref[pl.ds(place * count + chunk * unroll + at, 1), :] = mixed[pl.ds(source, 1), :]


VMEM = pl.BlockSpec(memory_space=pltpu.VMEM)
SMEM = pl.BlockSpec(memory_space=pltpu.SMEM)
MIB = 1024 * 1024


def picked_strip(slab, sign_bits, index, spot, groups, strip):
    height = slab.shape[0]
    samples = index.shape[0]
    half = jax.ShapeDtypeStruct((samples // 2, LANES), jnp.float32)
    table = jax.ShapeDtypeStruct((2 * height, LANES), jnp.float32)
    transform = functools.partial(transform_and_pick, groups, strip)
    if strip:
        kernel, out_shape, scratch = transform, (half, half), [pltpu.VMEM(table.shape, table.dtype)]
    else:
        kernel, out_shape, scratch = lambda *refs: transform(*refs[:4], None, *refs[4:]), (half, table), []
    first, second = pl.pallas_call(
        kernel,
        out_shape=out_shape,
        in_specs=[SMEM, SMEM, VMEM, VMEM],
        out_specs=(VMEM, VMEM),
        scratch_shapes=scratch,
        compiler_params=pltpu.CompilerParams(vmem_limit_bytes=32 * MIB),
        cost_estimate=pl.CostEstimate(
            flops=16 * height * INNER * LANES, bytes_accessed=16 * LANES * (height + samples), transcendentals=0
        ),
        name="transform_and_pick",
    )(spot, index, sign_bits, slab)
    if strip:
        return first, second
    keep = pl.pallas_call(
        functools.partial(gather, groups, 0),
        out_shape=half,
        in_specs=[SMEM, SMEM, VMEM],
        out_specs=VMEM,
        compiler_params=pltpu.CompilerParams(vmem_limit_bytes=32 * MIB),
        name="pick",
    )(spot, index, second)
    return keep, first


def two_parts(values):
    high = values.astype(jnp.bfloat16)
    return high, (values - high.astype(jnp.float32)).astype(jnp.bfloat16)


def three_products(left, right):
    dot = functools.partial(jnp.dot, preferred_element_type=jnp.float32)
    width = right[0].shape[1]
    both = dot(left[0], jnp.concatenate(right, axis=1))
    return both[:, :width] + both[:, width:] + dot(left[1], right[0])


def turn_plane(near, strips, spot_ref, *refs):
    parts, (high_ref, low_ref, own_ref) = refs[:-3], refs[-3:]
    width = own_ref.shape[1]
    for off in range(near):
        for strip in range(strips):
            high, low = two_parts(parts[off * strips + strip][...].T)
            where = pl.ds(pl.multiple_of((spot_ref[2] ^ off) * width + strip * LANES, LANES), LANES)
            high_ref[where, :] = high
            low_ref[where, :] = low
    own = jnp.concatenate([part[...] for part in parts[:strips]], axis=1)
    own_ref[...] = three_products((high_ref[...], low_ref[...]), two_parts(own))


def pair_products(groups, strip, flip, spot_ref, high_ref, low_ref, own_ref, *refs):
    remote, (keep_ref, send_ref) = refs[:-2], refs[-2:]
    me, at_plane = spot_ref[0], spot_ref[1]
    half = keep_ref.shape[0]
    bits = groups.bit_length() - 1
    back = 1 - 2 * (me & 1)

    def store(other, value):
        place = bit_reverse(other ^ me ^ flip, bits)

        @pl.when(place < half)
        def _():
            keep_ref[place] = value()

        @pl.when(place >= half)
        def _():
            send_ref[place - half] = value()

    store(at_plane, lambda: own_ref[:, strip * LANES : (strip + 1) * LANES])
    for away in range(1, groups):
        below, above = at_plane - away * back, at_plane + away * back

        @pl.when((below >= 0) & (below < groups))
        def _():
            product = three_products((high_ref[...], low_ref[...]), two_parts(remote[away - 1][...]))
            store(below, lambda: product)

        @pl.when((above >= 0) & (above < groups))
        def _():
            store(above, lambda: jnp.zeros(keep_ref.shape[1:], jnp.float32))


def finish(factor, strips, spot_ref, *refs):
    directs, turned, out_ref = refs[:strips], refs[strips:-1], refs[-1]
    width = out_ref.shape[1]
    for at, part in enumerate(turned):
        start = (spot_ref[2] ^ (at // strips)) * width + at % strips * LANES
        out_ref[pl.ds(pl.multiple_of(start, LANES), LANES), :] = part[...].T * factor

    @pl.when(spot_ref[0] != spot_ref[1])
    def _():
        direct = jnp.concatenate([part[...] for part in directs], axis=1)
        out_ref[...] = out_ref[...] + direct * factor


def shards(slab, sign_bits, sample_rows):
    height, width = slab.shape
    groups, columns = lax.axis_size("rows"), lax.axis_size("cols")
    near = columns // groups
    strips = width // LANES
    me, column = lax.axis_index("rows"), lax.axis_index("cols")
    samples = sample_rows.shape[0]
    factor = 1.0 / (samples * height * groups)
    bits = groups.bit_length() - 1

    owners = sample_rows // height
    common = owners & me
    parity = jnp.zeros_like(common)
    for at in range(bits):
        parity = parity ^ ((common >> at) & 1)
    index = sample_rows - owners * height + parity * height
    block = min(1024, height)
    sign_bits = sign_bits.reshape(height // block, block // INNER, INNER)
    spot = jnp.stack([me, column // near, column % near]).astype(jnp.int32)

    def halve(keep, send, at):
        got = lax.ppermute(send, "rows", [(r, r ^ (1 << at)) for r in range(groups)])
        half = keep.shape[0] // 2
        if at == bits - 1:
            return keep, got
        return keep[:half] + got[:half], keep[half:] + got[half:]

    def after(value, earlier):
        return lax.optimization_barrier((value, earlier))

    def onward(r, c):
        to = c + near if r % 2 == 0 else c - near
        return (r, to) if 0 <= to < columns else (r ^ 1, c)

    def pairs(to):
        ends = [(r, c, *to(r, c)) for r in range(groups) for c in range(columns)]
        return [(r * columns + c, r_to * columns + c_to) for r, c, r_to, c_to in ends]

    ring = pairs(onward)

    plane = [[] for _ in range(near)]
    remote, onward_parts = [], []
    for strip in range(strips):
        keep, send = picked_strip(slab, sign_bits, index, spot, groups, strip)
        if strip:
            send, plane[0][-1] = after(send, plane[0][-1])
        for at in range(bits):
            keep, send = halve(keep, send, at)
            if at == 0:
                index, send = after(index, send)
        if strip:
            send, remote[-1][0] = after(send, remote[-1][0])
            for side in plane[1:]:
                send, side[-1] = after(send, side[-1])
        own = keep + send
        moving, passed = own, []
        for away in range(1, groups - 1 if strip else groups):
            if strip and away > 1:
                moving, remote[-1][away - 1] = after(moving, remote[-1][away - 1])
            moving = lax.ppermute(moving, AXES, ring)
            passed.append(moving)
        if strip:
            moving, remote[-1][-1] = after(moving, remote[-1][-1])
        onward_parts.append(moving)
        remote.append(passed)
        plane[0].append(own)
        for off in range(1, near):
            plane[off].append(lax.ppermute(own, "cols", [(c, c ^ off) for c in range(columns)]))

    parts = [part for side in plane for part in side]
    depth = samples // groups
    turned = jax.ShapeDtypeStruct((near * width, depth), jnp.bfloat16)
    high, low, own_sums = pl.pallas_call(
        functools.partial(turn_plane, near, strips),
        out_shape=(turned, turned, jax.ShapeDtypeStruct((near * width, width), jnp.float32)),
        in_specs=[SMEM] + [VMEM] * len(parts),
        out_specs=(VMEM,) * 3,
        compiler_params=pltpu.CompilerParams(vmem_limit_bytes=32 * MIB),
        name="turn_plane",
    )(spot, *parts)

    half_sums = jax.ShapeDtypeStruct((groups // 2, near * width, LANES), jnp.float32)
    totals, directs, sideways = [], [], [[] for _ in range(near)]
    for strip in range(strips):
        flip = strip % 2 * (groups // 2)
        keep, send = pl.pallas_call(
            functools.partial(pair_products, groups, strip, flip),
            out_shape=(half_sums, half_sums),
            in_specs=[SMEM] + [VMEM] * (3 + len(remote[strip])),
            out_specs=(VMEM, VMEM),
            compiler_params=pltpu.CompilerParams(vmem_limit_bytes=32 * MIB),
            name="pair_products",
        )(spot, high, low, own_sums, *remote[strip])
        if strip + 1 < strips:
            moving, send = after(onward_parts[strip + 1], send)
            remote[strip + 1].append(lax.ppermute(moving, AXES, ring))
        if strip:
            send, totals[-1] = after(send, totals[-1])
        for at in range(bits):
            keep, send = halve(keep, send, at)
        if strip:
            for side in sideways[1:]:
                send, side[-1] = after(send, side[-1])
        total = (keep + send)[0]
        totals.append(total)
        directs.append(lax.ppermute(total, AXES, pairs(lambda r, c: (c // near, (r ^ flip) * near + c % near))))
        for off in range(near):
            part = lax.dynamic_slice_in_dim(total, (column % near ^ off) * width, width, 0)
            if off or flip:
                part = lax.ppermute(part, AXES, pairs(lambda r, c: (r ^ flip, c ^ off)))
            sideways[off].append(part)

    last = directs + [part for side in sideways for part in side]
    return pl.pallas_call(
        functools.partial(finish, factor, strips),
        out_shape=jax.ShapeDtypeStruct((near * width, width), jnp.float32),
        in_specs=[SMEM] + [VMEM] * len(last),
        out_specs=VMEM,
        compiler_params=pltpu.CompilerParams(vmem_limit_bytes=16 * MIB),
        name="finish",
    )(spot, *last)


def solution(mesh):
    return jax.shard_map(
        shards,
        mesh=mesh,
        in_specs=(P("rows", "cols"), P("rows"), P()),
        out_specs=P("rows", "cols"),
        check_vma=False,
    )
```
